32 devices in a mesh: grp: 4 (over z), nbr: 8 (over y, x, core).
Axes of the slice: x: 2, y: 2, z: 4, core: 2. Of those that a mesh axis runs over, the one named last changes fastest.
Arguments:
- fine_coef: bfloat16 [256, 1024], P(('grp', 'nbr')), may hold values from -6 to 6
- fine_live: int32 [32], P(('grp', 'nbr')), may hold values from 2 to 8, as said below
- fine_parent: int32 [256], P(('grp', 'nbr')), may hold values from 0 to 31, as said below
- up_transfer: bfloat16 [256, 1024], P(('grp', 'nbr')), may hold values from -1 to 1
- fine_list: int32 [256, 96], P(('grp', 'nbr')), may hold values from 0 to 255, as said below
- fine_nblk: int32 [256], P(('grp', 'nbr')), may hold values from 24 to 96, as said below
- fine_blocks: bfloat16 [256, 96, 1024], P(('grp', 'nbr')), may hold values from -1 to 1
- fine_scale: float32 [256, 96], P(('grp', 'nbr')), may hold values from 0.03 to 0.3
- coarse_list: int32 [32, 96], P(('grp', 'nbr')), may hold values from 0 to 31
- coarse_nblk: int32 [32], P(('grp', 'nbr')), may hold values from 24 to 96, as said below
- coarse_blocks: bfloat16 [32, 96, 1024], P(('grp', 'nbr')), may hold values from -1 to 1
- coarse_scale: float32 [32, 96], P(('grp', 'nbr')), may hold values from 0.01 to 0.1
- down_transfer: bfloat16 [256, 1024], P(('grp', 'nbr')), may hold values from -1 to 1
Outputs:
- fine_local: bfloat16 [256, 1024], P(('grp', 'nbr'))
The draws below stay inside these ranges and needn't reach their ends.
Inputs may be any that keep to these rules, and one draw needn't show every extreme that they name: `fine_live`: one owner in every draw holds all 8 slots. `fine_parent`: the parent of a fine slot lies in the same subtree group: slots g * 64 to (g + 1) * 64 - 1 have parents g * 8 to (g + 1) * 8 - 1. `fine_list`: every entry of a fine box's list is a live slot of the box's own subtree group. `fine_nblk`: some live box uses all 96 entries in every draw. `coarse_nblk`: some box uses all 96 entries in every draw.
All inputs are finite; a program needn't handle non-finite values.
Results may differ from the reference program's by a relative error of at most 0.0044.
Values may be sent and summed in bfloat16 or wider, within the bound.
A program may use at most 64 MiB of HBM per device.

```python
import math
import jax
import jax.numpy as jnp
from jax import lax

K = 32
R = 32
SF = 8
SC = 1
LIST = 96
LISTC = 96
NDEV = 32
NF = 256
NC = 32
GBOX = 64
GCOARSE = 8
N_NBR = 8


def live_counts(key):
    first, second = jax.random.split(jax.random.fold_in(key, 11))
    counts = jax.random.randint(first, (NDEV,), max(SF // 4, 1), SF + 1)
    fullest = jax.random.randint(second, (), 0, NDEV)
    return (counts.at[fullest].set(SF), fullest)


def draw_fine_live(key, part):
    return live_counts(key)[0].astype(jnp.int32)


def draw_fine_nblk(key, part):
    counts, fullest = live_counts(key)
    chosen = jax.random.fold_in(key, 12)
    used = jax.random.randint(chosen, (NF,), max(LIST // 4, 1), LIST + 1)
    return used.at[fullest * SF].set(LIST).astype(jnp.int32)


def draw_fine_list(key, part):
    counts, fullest = live_counts(key)
    first, second = jax.random.split(jax.random.fold_in(key, 13))
    group = jnp.arange(NF) // GBOX
    peer = jax.random.randint(first, (NF, LIST), 0, N_NBR)
    owner = group[:, None] * N_NBR + peer
    slot = jax.random.randint(second, (NF, LIST), 0, SF) % counts[owner]
    return (owner * SF + slot).astype(jnp.int32)


def draw_fine_parent(key, part):
    chosen = jax.random.fold_in(key, 14)
    group = jnp.arange(NF) // GBOX
    return (group * GCOARSE + jax.random.randint(chosen, (NF,), 0, GCOARSE)).astype(jnp.int32)


def draw_coarse_nblk(key, part):
    first, second = jax.random.split(jax.random.fold_in(key, 15))
    used = jax.random.randint(first, (NC,), max(LISTC // 4, 1), LISTC + 1)
    fullest = jax.random.randint(second, (), 0, NC)
    return used.at[fullest].set(LISTC).astype(jnp.int32)


def plant(values, rng, least, high):
    longest = values.shape.index(max(values.shape))
    spots = []
    for shift in (0, 1):
        where = [jax.random.randint(jax.random.fold_in(rng, axis), (), 0, length) for axis, length in enumerate(values.shape)]
        where[longest] = (where[longest] + shift) % values.shape[longest]
        spots.append(tuple(where))
    return values.at[spots[0]].set(least).at[spots[1]].set(high)


def shard_levels(stream_key, extent, pieces, smallest, top_value):
    loudness = 1.0
    for position, parts in pieces:
        steps = jax.random.uniform(jax.random.fold_in(jax.random.fold_in(stream_key, 6), position), (parts,), jnp.float32, smallest / len(pieces), top_value / len(pieces))
        loudness = loudness * jnp.repeat(jnp.exp(steps), extent[position] // parts).reshape((-1,) + (1,) * (len(extent) - 1 - position))
    return loudness


def noise(key, extent, width, limit, cuts=(), dtype=jnp.bfloat16):
    values = jax.random.normal(key, extent, jnp.float32) * width
    if len(cuts) > 0:
        values = shard_levels(key, extent, cuts, -0.22, 0.18) * values
    return jnp.clip(values, min=-limit, max=limit).astype(dtype)


def setup_inputs(seed: int = 0) -> dict:
    key_of = jax.random.split(jax.random.key(seed), 14)
    return {
        "fine_coef": noise(key_of[0], (NF, K * R), 1.0, 6.0, ((0, 32),)),
        "fine_live": draw_fine_live(jax.random.fold_in(key_of[13], 71), 0),
        "fine_parent": draw_fine_parent(jax.random.fold_in(key_of[13], 71), 0),
        "up_transfer": noise(key_of[3], (NF, K * K), K ** -0.5, 1.0, ((0, 32),)),
        "fine_list": draw_fine_list(jax.random.fold_in(key_of[13], 71), 0),
        "fine_nblk": draw_fine_nblk(jax.random.fold_in(key_of[13], 71), 0),
        "fine_blocks": noise(key_of[6], (NF, LIST, K * K), K ** -0.5, 1.0, ((0, 32),)),
        "fine_scale": jnp.clip(jnp.exp(math.log(0.3) - 2.3025852 * jax.random.uniform(key_of[7], (NF, LIST), jnp.float32) ** shard_levels(key_of[7], (NF, LIST), ((0, 32),), -0.2, 0.2)), 0.03, 0.3),
        "coarse_list": plant(jax.random.randint(key_of[8], (NC, LISTC), 0, NC), jax.random.fold_in(key_of[8], 1), 0, NC - 1).astype(jnp.int32),
        "coarse_nblk": draw_coarse_nblk(jax.random.fold_in(key_of[13], 71), 0),
        "coarse_blocks": noise(key_of[10], (NC, LISTC, K * K), K ** -0.5, 1.0, ((0, 32),)),
        "coarse_scale": jnp.clip(jnp.exp(math.log(0.1) - 2.3025851 * jax.random.uniform(key_of[11], (NC, LISTC), jnp.float32) ** shard_levels(key_of[11], (NC, LISTC), ((0, 32),), -0.2, 0.2)), 0.01, 0.1),
        "down_transfer": noise(key_of[12], (NF, K * K), K ** -0.5, 1.0, ((0, 32),)),
    }


def couple(blocks, scale, count, picked):
    prod = jnp.einsum("tjik,tjkr->tjir", blocks.astype(jnp.float32), picked.astype(jnp.float32))
    used = jnp.arange(scale.shape[1])[None, :] < count[:, None]
    weight = jnp.where(used, scale, jnp.float32(0.0))
    return jnp.sum(prod * weight[:, :, None, None], axis=1)


def reference(fine_coef, fine_live, fine_parent, up_transfer, fine_list, fine_nblk, fine_blocks, fine_scale, coarse_list, coarse_nblk, coarse_blocks, coarse_scale, down_transfer):
    live = (jnp.arange(NF) % SF) < jnp.repeat(fine_live, SF)
    source = jnp.where(live[:, None], fine_coef, jnp.zeros_like(fine_coef))
    lifted = jnp.einsum("bij,bjr->bir", up_transfer.reshape(NF, K, K).astype(jnp.float32), source.reshape(NF, K, R).astype(jnp.float32))
    coarse_coef = jax.ops.segment_sum(lifted, fine_parent, num_segments=NC).astype(jnp.bfloat16)

    def coarse_part(args):
        blocks, scale, count, listed = args
        picked = coarse_coef[listed]
        return couple(blocks.reshape(SC, LISTC, K, K), scale, count, picked)

    coarse_local = lax.map(coarse_part, (coarse_blocks.reshape(NDEV, SC, LISTC, K * K), coarse_scale.reshape(NDEV, SC, LISTC), coarse_nblk.reshape(NDEV, SC), coarse_list.reshape(NDEV, SC, LISTC)))
    coarse_local = coarse_local.reshape(NC, K, R).astype(jnp.bfloat16)

    source_boxes = source.reshape(NF, K, R)

    def fine_part(args):
        blocks, scale, count, listed = args
        picked = source_boxes[listed]
        return couple(blocks.reshape(SF, LIST, K, K), scale, count, picked)

    near = lax.map(fine_part, (fine_blocks.reshape(NDEV, SF, LIST, K * K), fine_scale.reshape(NDEV, SF, LIST), fine_nblk.reshape(NDEV, SF), fine_list.reshape(NDEV, SF, LIST)))
    near = near.reshape(NF, K, R)
    down = jnp.einsum("bij,bjr->bir", down_transfer.reshape(NF, K, K).astype(jnp.float32), coarse_local[fine_parent].astype(jnp.float32))
    total = jnp.where(live[:, None, None], near + down, jnp.float32(0.0))
    return total.reshape(NF, K * R).astype(jnp.bfloat16)
```

```python
import functools

import jax
import jax.numpy as jnp
from jax import lax
from jax.experimental import pallas as pl
from jax.experimental.pallas import tpu as pltpu
from jax.sharding import PartitionSpec as P

K = 32
R = 32
LANES = 128
ROWS = 8
PER = LANES // K
F32 = jnp.float32
BF16 = jnp.bfloat16
MESH = pl.DeviceIdType.MESH


def lane_group():
    return lax.broadcasted_iota(jnp.int32, (ROWS, LANES), 1) // K


def spread(tiles, scratch):
    group = lane_group()
    for q in range(ROWS):
        for m in range(PER):
            z = jnp.where(group == m, tiles[q], 0.0)
            z = z + pltpu.roll(z, K, 1)
            z = z + pltpu.roll(z, 2 * K, 1)
            scratch[pl.ds((PER * q + m) * ROWS, ROWS), :] = z
    return [scratch[pl.ds(s, K, stride=ROWS), :] for s in range(ROWS)]


def diagonal(boxes):
    group = lax.broadcasted_iota(jnp.int32, (K, LANES), 1) // K
    masks = [(group == i).astype(F32).astype(BF16) for i in range(PER)]
    rows = []
    for box in boxes:
        box = box.astype(BF16)
        rows.extend(box * mask for mask in masks)
    return jnp.concatenate(rows, axis=0)


def collect(listed, scale, count, blocks, base, sources):
    width = blocks.shape[0]
    used = lax.broadcasted_iota(jnp.int32, (1, width), 1) < count
    weight = jnp.where(used, scale, 0.0)
    high = weight.astype(BF16).astype(F32)
    low = weight - high
    hit = lax.broadcasted_iota(jnp.int32, (sources, width), 0) + base == listed
    left = jnp.concatenate(
        [jnp.where(hit, high, 0.0).astype(BF16), jnp.where(hit, low, 0.0).astype(BF16)], axis=1
    )
    right = jnp.concatenate([blocks, blocks], axis=0)
    return jnp.dot(left, right, preferred_element_type=F32)


def kernel(
    groups,
    members,
    live,
    parent,
    fnblk,
    cnblk,
    coef_h,
    up_h,
    flist_h,
    fscale_h,
    fblocks_h,
    clist_h,
    cscale_h,
    cblocks_h,
    down_h,
    out,
    coef,
    up,
    flist,
    fscale,
    fblocks,
    clist,
    cscale,
    cblocks,
    down,
    src_all,
    part,
    part_in,
    cc_all,
    cl_all,
    fine_c,
    coarse_c,
    turned_u,
    turned_d,
    turned_o,
    spread_s,
    spread_f,
    spread_c,
    spread_l,
    in_sem,
    src_send,
    src_recv,
    part_send,
    part_recv,
    cc_send,
    cc_recv,
    cl_send,
    cl_recv,
):
    ndev = groups * members
    slots = coef.shape[0]
    gbox = slots * members
    g = lax.axis_index("grp")
    n = lax.axis_index("nbr")
    me = g * members + n

    loads = [
        pltpu.make_async_copy(a, b, in_sem.at[i])
        for i, (a, b) in enumerate(
            [
                (coef_h, coef),
                (up_h, up),
                (flist_h, flist),
                (fscale_h, fscale),
                (fblocks_h, fblocks),
                (clist_h, clist),
                (cscale_h, cscale),
                (cblocks_h, cblocks),
                (down_h, down),
            ]
        )
    ]
    for load in loads:
        load.start()

    barrier = pltpu.get_barrier_semaphore()

    def everyone(act):
        def step(off, carry):
            other = lax.rem(me + off, ndev)
            act(other, (other // members, lax.rem(other, members)))
            return carry

        lax.fori_loop(1, ndev, step, 0)

    def group_of_mine(act):
        def step(off, carry):
            other = lax.rem(n + off, members)
            act(other, (g, other))
            return carry

        lax.fori_loop(1, members, step, 0)

    everyone(
        lambda other, where: pl.semaphore_signal(barrier, inc=1, device_id=where, device_id_type=MESH)
    )

    def settle(ref, count, sem):
        some = ref.at[pl.ds(0, count)]
        pltpu.make_async_copy(some, some, sem).wait()

    loads[0].wait()
    row = lax.broadcasted_iota(jnp.int32, (slots, 1), 0)
    source = jnp.where(row < live[0], coef[...].astype(F32), 0.0)
    half = source.shape[1] // 2
    src_all[n] = jnp.concatenate([source[:, :half], source[:, half:]], axis=0).astype(BF16)
    loads[1].wait()
    upf = up[...].astype(F32)
    for c in range(ROWS):
        turned_u[pl.ds(c * slots, slots), :] = upf[:, c * LANES : (c + 1) * LANES]
    own = diagonal(
        spread([source[:, q * LANES : (q + 1) * LANES] for q in range(ROWS)], spread_s)
    )
    ups = [turned_u[pl.ds(b, ROWS, stride=slots), :] for b in range(slots)]
    chunks = []
    for b in range(slots):
        mine = parent[b] - g * members
        chunks.append(
            jnp.concatenate(
                [jnp.where(mine == p, ups[b], 0.0) for p in range(members)], axis=0
            ).astype(BF16)
        )
    lifted = jnp.dot(jnp.concatenate(chunks, axis=1), own, preferred_element_type=F32)
    part[...] = lifted.reshape(members, ROWS, LANES)
    part_in[n] = part[n]

    pl.semaphore_wait(barrier, ndev - 1)

    def send_part(other, where):
        pltpu.make_async_remote_copy(
            part.at[other], part_in.at[n], part_send, part_recv, device_id=where, device_id_type=MESH
        ).start()

    def send_src(other, where):
        pltpu.make_async_remote_copy(
            src_all.at[n], src_all.at[n], src_send, src_recv, device_id=where, device_id_type=MESH
        ).start()

    group_of_mine(send_part)
    group_of_mine(send_src)

    for load in loads[5:8]:
        load.wait()
    found = collect(clist[...], cscale[...], cnblk[0], cblocks[0], 0, ndev)
    for c in range(ROWS):
        coarse_c[pl.ds(c * ndev, ndev), :] = found[:, c * LANES : (c + 1) * LANES]

    settle(part_in, members - 1, part_recv)
    coarse = part_in[0]
    for p in range(1, members):
        coarse = coarse + part_in[p]
    cc_all[me] = coarse.astype(BF16).astype(F32)

    def send_cc(other, where):
        pltpu.make_async_remote_copy(
            cc_all.at[me], cc_all.at[me], cc_send, cc_recv, device_id=where, device_id_type=MESH
        ).start()

    everyone(send_cc)

    for load in loads[2:5]:
        load.wait()
    for t in range(slots):
        found = collect(
            flist[pl.ds(t, 1), :], fscale[pl.ds(t, 1), :], fnblk[t], fblocks[t], g * gbox, gbox
        )
        for c in range(ROWS):
            fine_c[pl.ds((t * ROWS + c) * gbox, gbox), :] = found[:, c * LANES : (c + 1) * LANES]

    settle(cc_all, ndev - 1, cc_recv)

    def coarse_step(i, total):
        tiles = [cc_all[pl.ds(i * ROWS, ROWS), q, :] for q in range(ROWS)]
        right = diagonal(spread(tiles, spread_c.at[i]))
        left = jnp.concatenate(
            [coarse_c[pl.ds(i * ROWS + s, ROWS, stride=ndev), :].astype(BF16) for s in range(ROWS)],
            axis=1,
        )
        return total + jnp.dot(left, right, preferred_element_type=F32)

    local = lax.fori_loop(
        0, ndev // ROWS, coarse_step, jnp.zeros((ROWS, LANES), F32), unroll=ndev <= 32
    )
    cl_all[n] = local.astype(BF16).astype(F32)

    def send_cl(other, where):
        pltpu.make_async_remote_copy(
            cl_all.at[n], cl_all.at[n], cl_send, cl_recv, device_id=where, device_id_type=MESH
        ).start()

    group_of_mine(send_cl)

    settle(src_all, members - 1, src_recv)

    def near_step(i, total):
        block = src_all[i].astype(F32)
        tiles = [block[:ROWS, q * LANES : (q + 1) * LANES] for q in range(PER)]
        tiles += [block[ROWS:, q * LANES : (q + 1) * LANES] for q in range(PER)]
        right = diagonal(spread(tiles, spread_f.at[i]))
        left = jnp.concatenate(
            [
                fine_c[pl.ds(i * slots + s, slots * ROWS, stride=gbox), :].astype(BF16)
                for s in range(slots)
            ],
            axis=1,
        )
        return total + jnp.dot(left, right, preferred_element_type=F32)

    near = lax.fori_loop(
        0, members, near_step, jnp.zeros((slots * ROWS, LANES), F32), unroll=members <= 8
    )

    loads[8].wait()
    downf = down[...].astype(F32)
    for c in range(ROWS):
        turned_d[pl.ds(c * slots, slots), :] = downf[:, c * LANES : (c + 1) * LANES]
    downs = [turned_d[pl.ds(b, ROWS, stride=slots), :] for b in range(slots)]
    lefts = []
    for p in range(members):
        lefts.append(
            jnp.concatenate(
                [jnp.where(parent[b] - g * members == p, downs[b], 0.0) for b in range(slots)],
                axis=0,
            ).astype(BF16)
        )
    settle(cl_all, members - 1, cl_recv)
    total = near
    for i in range(members // ROWS):
        tiles = [cl_all[pl.ds(i * ROWS, ROWS), q, :] for q in range(ROWS)]
        right = diagonal(spread(tiles, spread_l.at[i]))
        left = jnp.concatenate(lefts[i * ROWS : (i + 1) * ROWS], axis=1)
        total = total + jnp.dot(left, right, preferred_element_type=F32)
    turned_o[...] = total
    keep = row < live[0]
    for c in range(ROWS):
        piece = turned_o[pl.ds(c, slots, stride=ROWS), :]
        out[:, c * LANES : (c + 1) * LANES] = jnp.where(keep, piece, 0.0).astype(BF16)

    settle(part_in, members - 1, part_send)
    settle(src_all, members - 1, src_send)
    settle(cc_all, ndev - 1, cc_send)
    settle(cl_all, members - 1, cl_send)


def body(
    fine_coef,
    fine_live,
    fine_parent,
    up_transfer,
    fine_list,
    fine_nblk,
    fine_blocks,
    fine_scale,
    coarse_list,
    coarse_nblk,
    coarse_blocks,
    coarse_scale,
    down_transfer,
):
    members = lax.axis_size("nbr")
    groups = lax.axis_size("grp")
    ndev = members * groups
    slots = fine_coef.shape[0]
    width = fine_list.shape[1]
    cwidth = coarse_list.shape[1]
    gbox = slots * members
    smem = pl.BlockSpec(memory_space=pltpu.SMEM)
    hbm = pl.BlockSpec(memory_space=pl.ANY)
    vm = pltpu.VMEM
    dma = pltpu.SemaphoreType.DMA
    flat = K * R
    return pl.pallas_call(
        functools.partial(kernel, groups, members),
        out_shape=jax.ShapeDtypeStruct((slots, flat), BF16),
        in_specs=[smem] * 4 + [hbm] * 9,
        out_specs=pl.BlockSpec(memory_space=pltpu.VMEM),
        scratch_shapes=[
            vm((slots, flat), BF16),
            vm((slots, flat), BF16),
            vm((slots, width), jnp.int32),
            vm((slots, width), F32),
            vm((slots, width, flat), BF16),
            vm((1, cwidth), jnp.int32),
            vm((1, cwidth), F32),
            vm((1, cwidth, flat), BF16),
            vm((slots, flat), BF16),
            vm((members, 2 * ROWS, flat // 2), BF16),
            vm((members, ROWS, LANES), F32),
            vm((members, ROWS, LANES), F32),
            vm((ndev, ROWS, LANES), F32),
            vm((members, ROWS, LANES), F32),
            vm((slots * ROWS * gbox, LANES), F32),
            vm((ROWS * ndev, LANES), F32),
            vm((ROWS * slots, LANES), F32),
            vm((ROWS * slots, LANES), F32),
            vm((ROWS * slots, LANES), F32),
            vm((K * ROWS, LANES), F32),
            vm((members, K * ROWS, LANES), F32),
            vm((ndev // ROWS, K * ROWS, LANES), F32),
            vm((members // ROWS, K * ROWS, LANES), F32),
            dma((9,)),
        ]
        + [dma] * 8,
        compiler_params=pltpu.CompilerParams(
            collective_id=0, has_side_effects=True, vmem_limit_bytes=40 * 1024 * 1024
        ),
    )(
        fine_live,
        fine_parent,
        fine_nblk,
        coarse_nblk,
        fine_coef,
        up_transfer,
        fine_list,
        fine_scale,
        fine_blocks,
        coarse_list,
        coarse_scale,
        coarse_blocks,
        down_transfer,
    )


def solution(mesh):
    rows = P(("grp", "nbr"), None)
    line = P(("grp", "nbr"))
    cube = P(("grp", "nbr"), None, None)
    placed = (rows, line, line, rows, rows, line, cube, rows, rows, line, cube, rows, rows)
    return jax.shard_map(body, mesh=mesh, in_specs=placed, out_specs=rows, check_vma=False)
```

```python
import functools

import jax
import jax.numpy as jnp
from jax import lax
from jax.experimental import pallas as pl
from jax.experimental.pallas import tpu as pltpu
from jax.sharding import PartitionSpec as P

K = 32
R = 32
LANES = 128
ROWS = 8
PER = LANES // K
F32 = jnp.float32
BF16 = jnp.bfloat16
MESH = pl.DeviceIdType.MESH


def lane_group():
    return lax.broadcasted_iota(jnp.int32, (ROWS, LANES), 1) // K


def spread(tiles, scratch):
    group = lane_group()
    for q in range(ROWS):
        for m in range(PER):
            z = jnp.where(group == m, tiles[q], 0.0)
            z = z + pltpu.roll(z, K, 1)
            z = z + pltpu.roll(z, 2 * K, 1)
            scratch[pl.ds((PER * q + m) * ROWS, ROWS), :] = z
    return [scratch[pl.ds(s, K, stride=ROWS), :] for s in range(ROWS)]


def diagonal(boxes):
    group = lax.broadcasted_iota(jnp.int32, (K, LANES), 1) // K
    masks = [(group == i).astype(F32).astype(BF16) for i in range(PER)]
    rows = []
    for box in boxes:
        box = box.astype(BF16)
        rows.extend(box * mask for mask in masks)
    return jnp.concatenate(rows, axis=0)


def collect(listed, scale, count, blocks, base, sources):
    width = blocks.shape[0]
    used = lax.broadcasted_iota(jnp.int32, (1, width), 1) < count
    weight = jnp.where(used, scale, 0.0)
    high = weight.astype(BF16).astype(F32)
    low = weight - high
    hit = lax.broadcasted_iota(jnp.int32, (sources, width), 0) + base == listed
    left = jnp.concatenate(
        [jnp.where(hit, high, 0.0).astype(BF16), jnp.where(hit, low, 0.0).astype(BF16)], axis=1
    )
    right = jnp.concatenate([blocks, blocks], axis=0)
    return jnp.dot(left, right, preferred_element_type=F32)


def kernel(
    groups,
    members,
    live_h,
    parent_h,
    fnblk_h,
    cnblk_h,
    coef_h,
    up_h,
    flist_h,
    fscale_h,
    fblocks_h,
    clist_h,
    cscale_h,
    cblocks_h,
    down_h,
    out,
    live,
    parent,
    fnblk,
    cnblk,
    coef,
    up,
    flist,
    fscale,
    fblocks,
    clist,
    cscale,
    cblocks,
    down,
    src_all,
    part,
    part_in,
    cc_all,
    cc_wide,
    cl_all,
    fine_c,
    coarse_c,
    turned_u,
    turned_d,
    turned_o,
    spread_s,
    spread_f,
    spread_c,
    spread_l,
    in_sem,
    src_send,
    src_recv,
    part_send,
    part_recv,
    cc_send,
    cc_recv,
    cl_send,
    cl_recv,
):
    ndev = groups * members
    slots = coef.shape[0]
    gbox = slots * members
    g = lax.axis_index("grp")
    n = lax.axis_index("nbr")
    me = g * members + n

    rank = [n] + [lax.rem(n + off, members) for off in range(1, members)]

    def columns(act):
        def step(off, carry):
            other = lax.rem(g + off, groups)
            act(other * members + n, (other, n))
            return carry

        lax.fori_loop(1, groups, step, 0, unroll=groups <= 4)

    def other_groups(act):
        def step(off, carry):
            other = lax.rem(g + off, groups)
            for m in range(members):
                act(other * members + rank[m], (other, rank[m]))
            return carry

        lax.fori_loop(1, groups, step, 0, unroll=groups <= 4)

    def group_of_mine(act):
        for off in range(1, members):
            act(rank[off], (g, rank[off]))

    barrier = pltpu.get_barrier_semaphore()

    def greet(other, where):
        pl.semaphore_signal(barrier, inc=1, device_id=where, device_id_type=MESH)

    group_of_mine(greet)
    columns(greet)

    loads = [
        pltpu.make_async_copy(a, b, in_sem.at[i])
        for i, (a, b) in enumerate(
            [
                (coef_h, coef),
                (up_h, up),
                (flist_h, flist),
                (fscale_h, fscale),
                (fblocks_h, fblocks),
                (clist_h, clist),
                (cscale_h, cscale),
                (cblocks_h, cblocks),
                (down_h, down),
                (live_h, live),
                (parent_h, parent),
                (fnblk_h, fnblk),
                (cnblk_h, cnblk),
            ]
        )
    ]
    for load in loads:
        load.start()

    def settle(ref, count, sem):
        some = ref.at[pl.ds(0, count)]
        pltpu.make_async_copy(some, some, sem).wait()

    for load in loads[9:]:
        load.wait()
    loads[0].wait()
    row = lax.broadcasted_iota(jnp.int32, (slots, 1), 0)
    source = jnp.where(row < live[0], coef[...].astype(F32), 0.0)
    half = source.shape[1] // 2
    src_all[n] = jnp.concatenate([source[:, :half], source[:, half:]], axis=0).astype(BF16)
    loads[1].wait()
    upf = up[...].astype(F32)
    for c in range(ROWS):
        turned_u[pl.ds(c * slots, slots), :] = upf[:, c * LANES : (c + 1) * LANES]
    own = diagonal(
        spread([source[:, q * LANES : (q + 1) * LANES] for q in range(ROWS)], spread_s)
    )
    ups = [turned_u[pl.ds(b, ROWS, stride=slots), :] for b in range(slots)]
    chunks = []
    for b in range(slots):
        mine = parent[b] - g * members
        chunks.append(
            jnp.concatenate(
                [jnp.where(mine == p, ups[b], 0.0) for p in range(members)], axis=0
            ).astype(BF16)
        )
    lifted = jnp.dot(jnp.concatenate(chunks, axis=1), own, preferred_element_type=F32)
    part[...] = lifted.reshape(members, ROWS, LANES)
    part_in[n] = part[n]

    pl.semaphore_wait(barrier, members + groups - 2)

    def send_part(other, where):
        pltpu.make_async_remote_copy(
            part.at[other], part_in.at[n], part_send, part_recv, device_id=where, device_id_type=MESH
        ).start()

    def send_src(other, where):
        pltpu.make_async_remote_copy(
            src_all.at[n], src_all.at[n], src_send, src_recv, device_id=where, device_id_type=MESH
        ).start()

    group_of_mine(send_part)
    group_of_mine(send_src)

    for load in loads[5:8]:
        load.wait()
    found = collect(clist[...], cscale[...], cnblk[0], cblocks[0], 0, ndev)
    for c in range(ROWS):
        coarse_c[pl.ds(c * ndev, ndev), :] = found[:, c * LANES : (c + 1) * LANES]

    settle(part_in, members - 1, part_recv)
    coarse = part_in[0]
    for p in range(1, members):
        coarse = coarse + part_in[p]
    cc_all[me] = coarse.astype(BF16)

    def send_cc(other, where):
        pltpu.make_async_remote_copy(
            cc_all.at[me], cc_all.at[me], cc_send, cc_recv, device_id=where, device_id_type=MESH
        ).start()

    other_groups(send_cc)
    group_of_mine(send_cc)

    for load in loads[2:5]:
        load.wait()
    for t in range(slots):
        found = collect(
            flist[pl.ds(t, 1), :], fscale[pl.ds(t, 1), :], fnblk[t], fblocks[t], g * gbox, gbox
        )
        for c in range(ROWS):
            fine_c[pl.ds((t * ROWS + c) * gbox, gbox), :] = found[:, c * LANES : (c + 1) * LANES]

    settle(cc_all, ndev - 1, cc_recv)

    def coarse_step(i, total):
        cc_wide[pl.ds(i * ROWS, ROWS)] = cc_all[pl.ds(i * ROWS, ROWS)].astype(F32)
        tiles = [cc_wide[pl.ds(i * ROWS, ROWS), q, :] for q in range(ROWS)]
        right = diagonal(spread(tiles, spread_c.at[i]))
        left = jnp.concatenate(
            [coarse_c[pl.ds(i * ROWS + s, ROWS, stride=ndev), :].astype(BF16) for s in range(ROWS)],
            axis=1,
        )
        return total + jnp.dot(left, right, preferred_element_type=F32)

    local = lax.fori_loop(
        0, ndev // ROWS, coarse_step, jnp.zeros((ROWS, LANES), F32), unroll=ndev <= 32
    )
    cl_all[n] = local.astype(BF16).astype(F32)

    def send_cl(other, where):
        pltpu.make_async_remote_copy(
            cl_all.at[n], cl_all.at[n], cl_send, cl_recv, device_id=where, device_id_type=MESH
        ).start()

    group_of_mine(send_cl)

    settle(src_all, members - 1, src_recv)

    def near_step(i, total):
        block = src_all[i].astype(F32)
        tiles = [block[:ROWS, q * LANES : (q + 1) * LANES] for q in range(PER)]
        tiles += [block[ROWS:, q * LANES : (q + 1) * LANES] for q in range(PER)]
        right = diagonal(spread(tiles, spread_f.at[i]))
        left = jnp.concatenate(
            [
                fine_c[pl.ds(i * slots + s, slots * ROWS, stride=gbox), :].astype(BF16)
                for s in range(slots)
            ],
            axis=1,
        )
        return total + jnp.dot(left, right, preferred_element_type=F32)

    near = lax.fori_loop(
        0, members, near_step, jnp.zeros((slots * ROWS, LANES), F32), unroll=members <= 8
    )

    loads[8].wait()
    downf = down[...].astype(F32)
    for c in range(ROWS):
        turned_d[pl.ds(c * slots, slots), :] = downf[:, c * LANES : (c + 1) * LANES]
    downs = [turned_d[pl.ds(b, ROWS, stride=slots), :] for b in range(slots)]
    lefts = []
    for p in range(members):
        lefts.append(
            jnp.concatenate(
                [jnp.where(parent[b] - g * members == p, downs[b], 0.0) for b in range(slots)],
                axis=0,
            ).astype(BF16)
        )
    settle(cl_all, members - 1, cl_recv)
    total = near
    for i in range(members // ROWS):
        tiles = [cl_all[pl.ds(i * ROWS, ROWS), q, :] for q in range(ROWS)]
        right = diagonal(spread(tiles, spread_l.at[i]))
        left = jnp.concatenate(lefts[i * ROWS : (i + 1) * ROWS], axis=1)
        total = total + jnp.dot(left, right, preferred_element_type=F32)
    turned_o[...] = total
    keep = row < live[0]
    for c in range(ROWS):
        piece = turned_o[pl.ds(c, slots, stride=ROWS), :]
        out[:, c * LANES : (c + 1) * LANES] = jnp.where(keep, piece, 0.0).astype(BF16)

    settle(part_in, members - 1, part_send)
    settle(src_all, members - 1, src_send)
    settle(cc_all, ndev - 1, cc_send)
    settle(cl_all, members - 1, cl_send)


def body(
    fine_coef,
    fine_live,
    fine_parent,
    up_transfer,
    fine_list,
    fine_nblk,
    fine_blocks,
    fine_scale,
    coarse_list,
    coarse_nblk,
    coarse_blocks,
    coarse_scale,
    down_transfer,
):
    members = lax.axis_size("nbr")
    groups = lax.axis_size("grp")
    ndev = members * groups
    slots = fine_coef.shape[0]
    width = fine_list.shape[1]
    cwidth = coarse_list.shape[1]
    gbox = slots * members
    hbm = pl.BlockSpec(memory_space=pltpu.HBM)
    vm = pltpu.VMEM
    dma = pltpu.SemaphoreType.DMA
    flat = K * R
    return pl.pallas_call(
        functools.partial(kernel, groups, members),
        out_shape=pltpu.VMEM((slots, flat), BF16),
        in_specs=[hbm] * 13,
        out_specs=pl.BlockSpec(memory_space=pltpu.VMEM),
        scratch_shapes=[
            pltpu.SMEM((1,), jnp.int32),
            pltpu.SMEM((slots,), jnp.int32),
            pltpu.SMEM((slots,), jnp.int32),
            pltpu.SMEM((1,), jnp.int32),
            vm((slots, flat), BF16),
            vm((slots, flat), BF16),
            vm((slots, width), jnp.int32),
            vm((slots, width), F32),
            vm((slots, width, flat), BF16),
            vm((1, cwidth), jnp.int32),
            vm((1, cwidth), F32),
            vm((1, cwidth, flat), BF16),
            vm((slots, flat), BF16),
            vm((members, 2 * ROWS, flat // 2), BF16),
            vm((members, ROWS, LANES), F32),
            vm((members, ROWS, LANES), F32),
            vm((ndev, ROWS, LANES), BF16),
            vm((ndev, ROWS, LANES), F32),
            vm((members, ROWS, LANES), F32),
            vm((slots * ROWS * gbox, LANES), F32),
            vm((ROWS * ndev, LANES), F32),
            vm((ROWS * slots, LANES), F32),
            vm((ROWS * slots, LANES), F32),
            vm((ROWS * slots, LANES), F32),
            vm((K * ROWS, LANES), F32),
            vm((members, K * ROWS, LANES), F32),
            vm((ndev // ROWS, K * ROWS, LANES), F32),
            vm((members // ROWS, K * ROWS, LANES), F32),
            dma((13,)),
        ]
        + [dma] * 8,
        compiler_params=pltpu.CompilerParams(
            collective_id=0, has_side_effects=True, vmem_limit_bytes=60 * 1024 * 1024
        ),
    )(
        fine_live,
        fine_parent,
        fine_nblk,
        coarse_nblk,
        fine_coef,
        up_transfer,
        fine_list,
        fine_scale,
        fine_blocks,
        coarse_list,
        coarse_scale,
        coarse_blocks,
        down_transfer,
    )


def solution(mesh):
    rows = P(("grp", "nbr"), None)
    line = P(("grp", "nbr"))
    cube = P(("grp", "nbr"), None, None)
    placed = (rows, line, line, rows, rows, line, cube, rows, rows, line, cube, rows, rows)
    return jax.shard_map(body, mesh=mesh, in_specs=placed, out_specs=rows, check_vma=False)
```

```python
import functools

import jax
import jax.numpy as jnp
from jax import lax
from jax.experimental import pallas as pl
from jax.experimental.pallas import tpu as pltpu
from jax.sharding import PartitionSpec as P

K = 32
R = 32
LANES = 128
ROWS = 8
PER = LANES // K
F32 = jnp.float32
BF16 = jnp.bfloat16
MESH = pl.DeviceIdType.MESH


def lane_group():
    return lax.broadcasted_iota(jnp.int32, (ROWS, LANES), 1) // K


def spread(tiles, scratch):
    group = lane_group()
    for q in range(ROWS):
        for m in range(PER):
            z = jnp.where(group == m, tiles[q], 0.0)
            z = z + pltpu.roll(z, K, 1)
            z = z + pltpu.roll(z, 2 * K, 1)
            scratch[pl.ds((PER * q + m) * ROWS, ROWS), :] = z
    return [scratch[pl.ds(s, K, stride=ROWS), :] for s in range(ROWS)]


def diagonal(boxes):
    group = lax.broadcasted_iota(jnp.int32, (K, LANES), 1) // K
    masks = [(group == i).astype(F32).astype(BF16) for i in range(PER)]
    rows = []
    for box in boxes:
        box = box.astype(BF16)
        rows.extend(box * mask for mask in masks)
    return jnp.concatenate(rows, axis=0)


def collect(listed, scale, count, blocks, base, sources):
    width = blocks.shape[0]
    used = lax.broadcasted_iota(jnp.int32, (1, width), 1) < count
    weight = jnp.where(used, scale, 0.0)
    high = weight.astype(BF16).astype(F32)
    low = weight - high
    hit = lax.broadcasted_iota(jnp.int32, (sources, width), 0) + base == listed
    left = jnp.concatenate(
        [jnp.where(hit, high, 0.0).astype(BF16), jnp.where(hit, low, 0.0).astype(BF16)], axis=1
    )
    right = jnp.concatenate([blocks, blocks], axis=0)
    return jnp.dot(left, right, preferred_element_type=F32)


def kernel(
    groups,
    members,
    live_h,
    parent_h,
    fnblk_h,
    cnblk_h,
    coef_h,
    up_h,
    flist_h,
    fscale_h,
    fblocks_h,
    clist_h,
    cscale_h,
    cblocks_h,
    down_h,
    out,
    live,
    parent,
    fnblk,
    cnblk,
    coef,
    up,
    flist,
    fscale,
    fblocks,
    clist,
    cscale,
    cblocks,
    down,
    src_all,
    part,
    part_in,
    cc_all,
    cc_wide,
    cl_all,
    fine_c,
    coarse_c,
    turned_u,
    turned_d,
    turned_o,
    spread_s,
    spread_f,
    spread_c,
    spread_l,
    in_sem,
    src_send,
    src_recv,
    part_send,
    part_recv,
    cc_send,
    cc_recv,
    cl_send,
    cl_recv,
):
    ndev = groups * members
    slots = coef.shape[0]
    gbox = slots * members
    g = lax.axis_index("grp")
    n = lax.axis_index("nbr")
    me = g * members + n

    rank = [n] + [lax.rem(n + off, members) for off in range(1, members)]

    def columns(act):
        def step(off, carry):
            other = lax.rem(g + off, groups)
            act(other * members + n, (other, n))
            return carry

        lax.fori_loop(1, groups, step, 0, unroll=groups <= 4)

    def other_groups(act):
        def step(off, carry):
            other = lax.rem(g + off, groups)
            for m in range(members):
                act(other * members + rank[m], (other, rank[m]))
            return carry

        lax.fori_loop(1, groups, step, 0, unroll=groups <= 4)

    def group_of_mine(act):
        for off in range(1, members):
            act(rank[off], (g, rank[off]))

    loads = [
        pltpu.make_async_copy(a, b, in_sem.at[i])
        for i, (a, b) in enumerate(
            [
                (coef_h, coef),
                (up_h, up),
                (flist_h, flist),
                (fscale_h, fscale),
                (fblocks_h, fblocks),
                (clist_h, clist),
                (cscale_h, cscale),
                (cblocks_h, cblocks),
                (down_h, down),
                (live_h, live),
                (parent_h, parent),
                (fnblk_h, fnblk),
                (cnblk_h, cnblk),
            ]
        )
    ]
    first = [loads[i] for i in (9, 10, 0, 1)]
    for load in first:
        load.start()

    barrier = pltpu.get_barrier_semaphore()

    def greet(other, where):
        pl.semaphore_signal(barrier, inc=1, device_id=where, device_id_type=MESH)

    group_of_mine(greet)
    columns(greet)


    def settle(ref, count, sem):
        some = ref.at[pl.ds(0, count)]
        pltpu.make_async_copy(some, some, sem).wait()

    loads[9].wait()
    loads[0].wait()
    row = lax.broadcasted_iota(jnp.int32, (slots, 1), 0)
    source = jnp.where(row < live[0], coef[...].astype(F32), 0.0)
    half = source.shape[1] // 2
    src_all[n] = jnp.concatenate([source[:, :half], source[:, half:]], axis=0).astype(BF16)
    loads[1].wait()
    loads[10].wait()
    upf = up[...].astype(F32)
    for c in range(ROWS):
        turned_u[pl.ds(c * slots, slots), :] = upf[:, c * LANES : (c + 1) * LANES]
    own = diagonal(
        spread([source[:, q * LANES : (q + 1) * LANES] for q in range(ROWS)], spread_s)
    )
    ups = [turned_u[pl.ds(b, ROWS, stride=slots), :] for b in range(slots)]
    chunks = []
    for b in range(slots):
        mine = parent[b] - g * members
        chunks.append(
            jnp.concatenate(
                [jnp.where(mine == p, ups[b], 0.0) for p in range(members)], axis=0
            ).astype(BF16)
        )
    lifted = jnp.dot(jnp.concatenate(chunks, axis=1), own, preferred_element_type=F32)
    part[...] = lifted.reshape(members, ROWS, LANES)
    part_in[n] = part[n]

    pl.semaphore_wait(barrier, members + groups - 2)

    def send_part(other, where):
        pltpu.make_async_remote_copy(
            part.at[other], part_in.at[n], part_send, part_recv, device_id=where, device_id_type=MESH
        ).start()

    def send_src(other, where):
        pltpu.make_async_remote_copy(
            src_all.at[n], src_all.at[n], src_send, src_recv, device_id=where, device_id_type=MESH
        ).start()

    group_of_mine(send_part)
    group_of_mine(send_src)
    for i in (5, 6, 7, 12, 2, 3, 11, 4, 8):
        loads[i].start()

    for i in (5, 6, 7, 12):
        loads[i].wait()
    found = collect(clist[...], cscale[...], cnblk[0], cblocks[0], 0, ndev)
    for c in range(ROWS):
        coarse_c[pl.ds(c * ndev, ndev), :] = found[:, c * LANES : (c + 1) * LANES]

    settle(part_in, members - 1, part_recv)
    coarse = part_in[0]
    for p in range(1, members):
        coarse = coarse + part_in[p]
    cc_all[me] = coarse.astype(BF16)

    def send_cc(other, where):
        pltpu.make_async_remote_copy(
            cc_all.at[me], cc_all.at[me], cc_send, cc_recv, device_id=where, device_id_type=MESH
        ).start()

    other_groups(send_cc)
    group_of_mine(send_cc)

    for i in (2, 3, 11, 4):
        loads[i].wait()
    for t in range(slots):
        found = collect(
            flist[pl.ds(t, 1), :], fscale[pl.ds(t, 1), :], fnblk[t], fblocks[t], g * gbox, gbox
        )
        for c in range(ROWS):
            fine_c[pl.ds((t * ROWS + c) * gbox, gbox), :] = found[:, c * LANES : (c + 1) * LANES]

    settle(cc_all, ndev - 1, cc_recv)

    def coarse_step(i, total):
        cc_wide[pl.ds(i * ROWS, ROWS)] = cc_all[pl.ds(i * ROWS, ROWS)].astype(F32)
        tiles = [cc_wide[pl.ds(i * ROWS, ROWS), q, :] for q in range(ROWS)]
        right = diagonal(spread(tiles, spread_c.at[i]))
        left = jnp.concatenate(
            [coarse_c[pl.ds(i * ROWS + s, ROWS, stride=ndev), :].astype(BF16) for s in range(ROWS)],
            axis=1,
        )
        return total + jnp.dot(left, right, preferred_element_type=F32)

    local = lax.fori_loop(
        0, ndev // ROWS, coarse_step, jnp.zeros((ROWS, LANES), F32), unroll=ndev <= 32
    )
    cl_all[n] = local.astype(BF16).astype(F32)

    def send_cl(other, where):
        pltpu.make_async_remote_copy(
            cl_all.at[n], cl_all.at[n], cl_send, cl_recv, device_id=where, device_id_type=MESH
        ).start()

    group_of_mine(send_cl)

    settle(src_all, members - 1, src_recv)

    def near_step(i, total):
        block = src_all[i].astype(F32)
        tiles = [block[:ROWS, q * LANES : (q + 1) * LANES] for q in range(PER)]
        tiles += [block[ROWS:, q * LANES : (q + 1) * LANES] for q in range(PER)]
        right = diagonal(spread(tiles, spread_f.at[i]))
        left = jnp.concatenate(
            [
                fine_c[pl.ds(i * slots + s, slots * ROWS, stride=gbox), :].astype(BF16)
                for s in range(slots)
            ],
            axis=1,
        )
        return total + jnp.dot(left, right, preferred_element_type=F32)

    near = lax.fori_loop(
        0, members, near_step, jnp.zeros((slots * ROWS, LANES), F32), unroll=members <= 8
    )

    loads[8].wait()
    downf = down[...].astype(F32)
    for c in range(ROWS):
        turned_d[pl.ds(c * slots, slots), :] = downf[:, c * LANES : (c + 1) * LANES]
    downs = [turned_d[pl.ds(b, ROWS, stride=slots), :] for b in range(slots)]
    lefts = []
    for p in range(members):
        lefts.append(
            jnp.concatenate(
                [jnp.where(parent[b] - g * members == p, downs[b], 0.0) for b in range(slots)],
                axis=0,
            ).astype(BF16)
        )
    settle(cl_all, members - 1, cl_recv)
    total = near
    for i in range(members // ROWS):
        tiles = [cl_all[pl.ds(i * ROWS, ROWS), q, :] for q in range(ROWS)]
        right = diagonal(spread(tiles, spread_l.at[i]))
        left = jnp.concatenate(lefts[i * ROWS : (i + 1) * ROWS], axis=1)
        total = total + jnp.dot(left, right, preferred_element_type=F32)
    turned_o[...] = total
    keep = row < live[0]
    for c in range(ROWS):
        piece = turned_o[pl.ds(c, slots, stride=ROWS), :]
        out[:, c * LANES : (c + 1) * LANES] = jnp.where(keep, piece, 0.0).astype(BF16)

    settle(part_in, members - 1, part_send)
    settle(src_all, members - 1, src_send)
    settle(cc_all, ndev - 1, cc_send)
    settle(cl_all, members - 1, cl_send)


def body(
    fine_coef,
    fine_live,
    fine_parent,
    up_transfer,
    fine_list,
    fine_nblk,
    fine_blocks,
    fine_scale,
    coarse_list,
    coarse_nblk,
    coarse_blocks,
    coarse_scale,
    down_transfer,
):
    members = lax.axis_size("nbr")
    groups = lax.axis_size("grp")
    ndev = members * groups
    slots = fine_coef.shape[0]
    width = fine_list.shape[1]
    cwidth = coarse_list.shape[1]
    gbox = slots * members
    hbm = pl.BlockSpec(memory_space=pltpu.HBM)
    vm = pltpu.VMEM
    dma = pltpu.SemaphoreType.DMA
    flat = K * R
    return pl.pallas_call(
        functools.partial(kernel, groups, members),
        out_shape=pltpu.VMEM((slots, flat), BF16),
        in_specs=[hbm] * 13,
        out_specs=pl.BlockSpec(memory_space=pltpu.VMEM),
        scratch_shapes=[
            pltpu.SMEM((1,), jnp.int32),
            pltpu.SMEM((slots,), jnp.int32),
            pltpu.SMEM((slots,), jnp.int32),
            pltpu.SMEM((1,), jnp.int32),
            vm((slots, flat), BF16),
            vm((slots, flat), BF16),
            vm((slots, width), jnp.int32),
            vm((slots, width), F32),
            vm((slots, width, flat), BF16),
            vm((1, cwidth), jnp.int32),
            vm((1, cwidth), F32),
            vm((1, cwidth, flat), BF16),
            vm((slots, flat), BF16),
            vm((members, 2 * ROWS, flat // 2), BF16),
            vm((members, ROWS, LANES), F32),
            vm((members, ROWS, LANES), F32),
            vm((ndev, ROWS, LANES), BF16),
            vm((ndev, ROWS, LANES), F32),
            vm((members, ROWS, LANES), F32),
            vm((slots * ROWS * gbox, LANES), F32),
            vm((ROWS * ndev, LANES), F32),
            vm((ROWS * slots, LANES), F32),
            vm((ROWS * slots, LANES), F32),
            vm((ROWS * slots, LANES), F32),
            vm((K * ROWS, LANES), F32),
            vm((members, K * ROWS, LANES), F32),
            vm((ndev // ROWS, K * ROWS, LANES), F32),
            vm((members // ROWS, K * ROWS, LANES), F32),
            dma((13,)),
        ]
        + [dma] * 8,
        compiler_params=pltpu.CompilerParams(
            collective_id=0, has_side_effects=True, vmem_limit_bytes=60 * 1024 * 1024
        ),
    )(
        fine_live,
        fine_parent,
        fine_nblk,
        coarse_nblk,
        fine_coef,
        up_transfer,
        fine_list,
        fine_scale,
        fine_blocks,
        coarse_list,
        coarse_scale,
        coarse_blocks,
        down_transfer,
    )


def solution(mesh):
    rows = P(("grp", "nbr"), None)
    line = P(("grp", "nbr"))
    cube = P(("grp", "nbr"), None, None)
    placed = (rows, line, line, rows, rows, line, cube, rows, rows, line, cube, rows, rows)
    return jax.shard_map(body, mesh=mesh, in_specs=placed, out_specs=rows, check_vma=False)
```
